512 devices in a mesh: row: 16 (over z_lo, x), col: 32 (over z_hi, y, core).
Axes of the slice: x: 4, y: 8, z: 8 (z_hi: 2, z_lo: 4; z = z_hi * 4 + z_lo), core: 2. Of those that a mesh axis runs over, the one named last changes fastest.
Arguments:
- ppmi_tiles: bfloat16 [1, 16, 512, 256, 256], P(None, 'row', 'col')
- tile_map: int32 [1, 16, 32, 16], P(None, 'row', 'col'), may hold values from 0 to 15, each once within a row
- sketch: bfloat16 [131072, 128], P(('col', 'row')), may hold values from -6 to 6
Outputs:
- q_basis: float32 [131072, 128], P(('col', 'row'))
The draws below stay inside these ranges and needn't reach their ends.
Inputs may be any that keep to these rules, and one draw needn't show every extreme that they name: For every k, r, c the entries tile_map[k, r, c, :] are each of 0 to 15 once.
All inputs are finite; a program needn't handle non-finite values.
Results may differ from the reference program's by a relative error of at most 0.0065.
Values may be sent and summed in bfloat16 or wider, within the bound.
No kernel may reach another device: no remote copies, remote signals or barrier semaphores. Data moves between devices by JAX's collectives and lax.ppermute only.
A program may use at most 64 MiB of HBM per device.

```python
import jax
import jax.numpy as jnp
from jax import lax

TILE = 256
SKETCH = 128
BAND_DEV = 1
SLOTS = 16
NBLK = 512
VOCAB = 131072
N_ROW = 16
N_COL = 32


def draw_ppmi_tiles(key, part):
    key = jax.random.fold_in(key, 11)
    value_key, row_key, col_key = jax.random.split(key, 3)
    full_shape = (BAND_DEV, N_ROW, N_COL * N_ROW, TILE, TILE)
    row_scale = 10.0 ** (0.5 * jax.random.uniform(row_key, full_shape[:-1] + (1,), jnp.float32))
    col_scale = 10.0 ** (0.5 * jax.random.uniform(col_key, full_shape[:-2] + (1, TILE), jnp.float32))
    values = jax.random.normal(value_key, full_shape, jnp.float32)
    return (0.3 * values * row_scale * col_scale).astype(jnp.bfloat16)


def block_levels(own_key, shape, shards, low, top_value):
    gain, own = 1.0, jax.random.fold_in(own_key, 6)
    for position, blocks in shards:
        heights = jnp.exp(jax.random.uniform(jax.random.fold_in(own, position), (blocks,), jnp.float32, low / len(shards), top_value / len(shards)))
        gain = gain * jnp.repeat(heights, shape[position] // blocks).reshape([-1 if axis == position else 1 for axis in range(len(shape))])
    return gain


def gaussian(stream_key, extent, width, reach, cuts=(), held_as=jnp.bfloat16):
    factor_of = block_levels(stream_key, extent, cuts, -0.22, 0.18) if cuts else 1.0
    entries = jax.random.normal(stream_key, extent, jnp.float32) * width * factor_of
    return jnp.minimum(jnp.maximum(entries, -reach), reach).astype(held_as)


def setup_inputs(seed: int = 0) -> dict:
    arg_keys = jax.random.split(jax.random.key(seed), 4)
    return {
        "ppmi_tiles": draw_ppmi_tiles(jax.random.fold_in(arg_keys[3], 71), 0),
        "tile_map": jax.vmap(lambda own: jax.random.permutation(own, N_ROW))(jax.random.split(arg_keys[1], BAND_DEV * N_ROW * N_COL)).reshape((BAND_DEV, N_ROW, N_COL, N_ROW)).astype(jnp.int32),
        "sketch": gaussian(arg_keys[2], (VOCAB, SKETCH), 1.0, 6.0, ((0, 512),)),
    }


def one_pass(ppmi_tiles, tile_map, basis_in):
    groups = NBLK // SLOTS
    band_count = ppmi_tiles.shape[0]
    blocks = basis_in.reshape(NBLK, TILE, SKETCH)

    def advance(totals, counter):
        band_k = counter // SLOTS
        band_r = counter % SLOTS
        band = (band_r + SLOTS * band_k).astype(jnp.int32)
        columns = (SLOTS * jnp.arange(groups, dtype=jnp.int32)[:, None] + tile_map[band_k, band_r]).reshape(-1).astype(jnp.int32)
        tile_f32 = ppmi_tiles[band_k, band_r].astype(jnp.float32)
        keep_mask = (columns >= band).astype(jnp.float32)
        strict = (columns > band).astype(jnp.float32)
        diag_weight = (columns == band).astype(jnp.float32)
        near_blocks = blocks[columns].astype(jnp.float32) * keep_mask[:, None, None]
        own_block = blocks[band].astype(jnp.float32)
        row_part = jnp.einsum('jab,jbn->an', tile_f32, near_blocks)
        diagonal = jnp.einsum('jab,j->ab', tile_f32, diag_weight)
        correction = jnp.triu(diagonal, 1).T - jnp.tril(diagonal, -1)
        row_part = row_part + jnp.dot(correction.astype(jnp.float32), own_block.astype(jnp.float32), preferred_element_type=jnp.float32)
        col_part = jnp.einsum('jab,an->jbn', tile_f32, own_block) * strict[:, None, None]
        totals = totals.at[columns].add(col_part)
        totals = totals.at[band].add(row_part)
        return (totals, None)
    start = jnp.zeros((NBLK, TILE, SKETCH), jnp.float32)
    totals, _ = lax.scan(advance, start, jnp.arange(band_count * SLOTS, dtype=jnp.int32))
    stacked = totals.reshape(NBLK * TILE, SKETCH)
    gram_matrix = jnp.dot(stacked.T, stacked, precision=lax.Precision.HIGHEST)
    factor = jnp.linalg.cholesky(gram_matrix)
    return jax.scipy.linalg.solve_triangular(factor, stacked.T, lower=True).T

def reference(ppmi_tiles, tile_map, sketch):
    basis = one_pass(ppmi_tiles, tile_map, sketch).astype(jnp.bfloat16)
    return one_pass(ppmi_tiles, tile_map, basis)
```

```python
import jax
import jax.numpy as jnp
from jax import lax
from jax.sharding import Mesh, PartitionSpec as P

ROW = ("zl", "x")
COL = ("zh", "y", "core")
HIGHEST = lax.Precision.HIGHEST


def swap(value, axes):
    return lax.all_to_all(value, axes, 0, 0, tiled=True)


def gather_row(block):
    return swap(jnp.broadcast_to(block[None], (16,) + block.shape), ROW)


def from_first_column(block):
    with jax.named_scope("sketch_to_columns"):
        other = lax.ppermute(block, "zh", [(0, 1)])
        block = jnp.where(lax.axis_index("zh") == 0, block, other)
        block = swap(jnp.broadcast_to(block[None], (8,) + block.shape), "y")[0]
        other = lax.ppermute(block, "core", [(0, 1)])
        return jnp.where(lax.axis_index("core") == 0, block, other)


def multiply(tiles, columns, band_id, near, band_block):
    keep = (columns >= band_id).astype(jnp.bfloat16)
    strict = (columns > band_id).astype(jnp.float32)
    row_part = jnp.einsum(
        "tab,tbn->an", tiles, near * keep[:, None, None], preferred_element_type=jnp.float32
    )
    products = jnp.einsum("tab,an->tbn", tiles, band_block, preferred_element_type=jnp.float32)
    return row_part, products * strict[:, None, None]


def one_pass(tiles, slots, inverse, correction, own, band_block):
    row_id, col_id = lax.axis_index(ROW), lax.axis_index(COL)
    columns = 16 * col_id + slots
    blocks = gather_row(own)
    near = jnp.take(blocks, slots, axis=0)
    row_part, products = multiply(tiles, columns, row_id, near, band_block)
    row_part = row_part + jnp.dot(correction, own, preferred_element_type=jnp.float32)
    placed = jnp.take(products, inverse, axis=0).astype(jnp.bfloat16)
    received = swap(placed, ROW)
    col_sum = jnp.sum(received.astype(jnp.float32), axis=0)
    first_col = col_id == 0
    row_part = row_part + jnp.where(first_col, col_sum, 0.0)
    rest = jnp.where(first_col, 0.0, col_sum)
    band_rows = jnp.sum(swap(row_part.reshape(32, 8, 128), COL), axis=0)
    stacked = jnp.concatenate([rest, band_rows], axis=0)
    gram = jnp.dot(stacked.T, stacked, precision=HIGHEST)
    piece = jnp.sum(swap(gram.reshape(16, 8, 128), ROW), axis=0)
    both = jnp.concatenate([piece, band_rows], axis=0)
    both = swap(jnp.broadcast_to(both[None], (32, 16, 128)), COL)
    piece = jnp.sum(both[:, :8], axis=0)
    band = both[:, 8:].reshape(256, 128)
    gram = gather_row(piece).reshape(128, 128)
    factor = jnp.linalg.cholesky(gram)
    own = jnp.where(first_col, band, rest)
    return factor, own, band


def local(ppmi_tiles, tile_map, sketch):
    row_id, col_id = lax.axis_index(ROW), lax.axis_index(COL)
    tiles = ppmi_tiles[0, 0]
    slots = tile_map[0, 0, 0]
    inverse = jnp.argmax(slots[None, :] == jnp.arange(16)[:, None], axis=1)
    is_diag = 16 * col_id + slots == row_id
    diag = tiles[jnp.argmax(is_diag)]
    correction = jnp.swapaxes(jnp.triu(diag, 1), 0, 1) - jnp.tril(diag, -1)
    correction = correction * jnp.any(is_diag).astype(jnp.bfloat16)
    band_block = from_first_column(sketch)
    factor, own, band = one_pass(tiles, slots, inverse, correction, sketch, band_block)
    wide = jnp.concatenate([own, band], axis=0)
    basis = jax.scipy.linalg.solve_triangular(factor, wide.T, lower=True).T.astype(jnp.bfloat16)
    factor, own, _ = one_pass(tiles, slots, inverse, correction, basis[:256], basis[256:])
    return jax.scipy.linalg.solve_triangular(factor, own.T, lower=True).T


def solution(mesh):
    fine = Mesh(mesh.devices.reshape(4, 4, 2, 8, 2), ROW + COL)
    in_specs = (
        P(None, ROW, COL, None, None),
        P(None, ROW, COL, None),
        P(COL + ROW, None),
    )
    return jax.shard_map(
        local, mesh=fine, in_specs=in_specs, out_specs=P(COL + ROW, None), check_vma=False
    )
```

```python
import functools

import jax
import jax.numpy as jnp
from jax import lax
from jax.experimental import pallas as pl
from jax.experimental.pallas import tpu as pltpu
from jax.sharding import Mesh, PartitionSpec as P

ROW = ("zl", "x")
COL = ("zh", "y", "core")
HIGHEST = lax.Precision.HIGHEST
PANEL = 32


def swap(value, axes):
    return lax.all_to_all(value, axes, 0, 0, tiled=True)


def copies_of(block, count):
    return jnp.broadcast_to(block[None], (count,) + block.shape)


FAR = [[(0, 4)], [(0, 8)], [(0, 12)]]
NEAR = [[(0, 1), (4, 5)], [(0, 7), (4, 3)], [(0, 2), (4, 6)]]


def backward(pairs):
    return [(target, source) for source, target in pairs]


def from_first_column(block):
    zh, y, core = (lax.axis_index(axis) for axis in COL)
    far = sum(lax.ppermute(block, ("zh", "y"), pairs) for pairs in FAR)
    block = jnp.where((zh == 0) & (y == 0), block, far)
    near = sum(lax.ppermute(block, "y", pairs) for pairs in NEAR)
    block = jnp.where(y % 4 == 0, block, near)
    other = lax.ppermute(block, "core", [(0, 1)])
    return jnp.where(core == 0, block, other)


def to_first_column(value):
    half = value.shape[0] // 2
    core = lax.axis_index("core")
    given = lax.dynamic_slice_in_dim(value, (1 - core) * half, half)
    value = lax.dynamic_slice_in_dim(value, core * half, half)
    value = value + lax.ppermute(given, "core", [(0, 1), (1, 0)])
    value = value + sum(lax.ppermute(value, "y", backward(pairs)) for pairs in NEAR)
    value = value + sum(lax.ppermute(value, ("zh", "y"), backward(pairs)) for pairs in FAR)
    return jnp.concatenate([value, lax.ppermute(value, "core", [(1, 0)])], axis=0)


VMEM = pl.BlockSpec(memory_space=pltpu.VMEM)
SMEM = pl.BlockSpec(memory_space=pltpu.SMEM)


def column_kernel(by_x, slots_ref, place_ref, tiles_ref, band_ref, out_ref):
    band = band_ref[...]

    def one(t, carry):
        slot = slots_ref[t]
        product = lax.dot_general(
            tiles_ref[t], band, (((0,), (0,)), ((), ())), preferred_element_type=jnp.float32
        )
        where = lax.rem(slot, 4) * 4 + lax.div(slot, 4) if by_x else slot
        out_ref[where] = jnp.where(slot > place_ref[0], product, 0.0).astype(jnp.bfloat16)
        return carry

    lax.fori_loop(0, tiles_ref.shape[0], one, 0, unroll=4)


def column_products(tiles, slots, place, band_block, by_x):
    count, tile = tiles.shape[:2]
    shape = (count, tile, band_block.shape[1])
    return pl.pallas_call(
        functools.partial(column_kernel, by_x),
        out_shape=jax.ShapeDtypeStruct(shape, jnp.bfloat16),
        in_specs=[SMEM, SMEM, VMEM, VMEM],
        out_specs=VMEM,
        cost_estimate=pl.CostEstimate(
            flops=2 * count * tile * tile * shape[2], bytes_accessed=1 << 23, transcendentals=0
        ),
        name="column_products",
    )(slots, place, tiles, band_block)


def normalise_kernel(gram_ref, wide_ref, out_ref, inverse_ref, work):
    size = gram_ref.shape[0]
    work[:, :size] = gram_ref[...]
    down = lax.broadcasted_iota(jnp.int32, (size, size), 0)
    across = lax.broadcasted_iota(jnp.int32, (size, size), 1)
    work[:, size:] = (down == across).astype(jnp.float32)
    rows = lax.broadcasted_iota(jnp.int32, (PANEL, size), 0)
    for start in range(0, size, PANEL):
        left = work[start : start + PANEL, :size]
        right = work[start : start + PANEL, size:]
        lanes = [
            jnp.broadcast_to(left[:, start + j : start + j + 1], (PANEL, size))
            for j in range(PANEL)
        ]
        for k in range(PANEL):
            pivot = jnp.broadcast_to(lanes[k][k : k + 1], (PANEL, size))
            scale = lax.rsqrt(pivot)
            scale = scale * (1.5 - 0.5 * pivot * scale * scale)
            below = jnp.where(rows > k, lanes[k] * scale, 0.0)
            for j in range(k + 1, PANEL):
                lanes[j] = lanes[j] - below * jnp.broadcast_to(below[j : j + 1], (PANEL, size))
            line = left[k : k + 1] * scale[k : k + 1]
            left = jnp.where(rows == k, line, left - below * line)
            line = right[k : k + 1] * scale[k : k + 1]
            right = jnp.where(rows == k, line, right - below * line)
        both = jnp.concatenate([left, right], axis=1)
        work[start : start + PANEL, :] = both
        after = start + PANEL
        if after < size:
            update = lax.dot_general(
                left,
                both,
                (((0,), (0,)), ((), ())),
                precision=HIGHEST,
                preferred_element_type=jnp.float32,
            )
            work[after:, :] = work[after:, :] - update[after:, :]
    out = lax.dot_general(
        wide_ref[...],
        work[:, size:],
        (((1,), (1,)), ((), ())),
        precision=HIGHEST,
        preferred_element_type=jnp.float32,
    )
    out_ref[...] = out.astype(out_ref.dtype)
    inverse_ref[...] = work[:, size:]


def normalise(gram, wide, dtype):
    size = gram.shape[0]
    return pl.pallas_call(
        normalise_kernel,
        out_shape=(
            jax.ShapeDtypeStruct(wide.shape, dtype),
            jax.ShapeDtypeStruct(gram.shape, jnp.float32),
        ),
        in_specs=[pl.BlockSpec(memory_space=pltpu.VMEM)] * 2,
        out_specs=[pl.BlockSpec(memory_space=pltpu.VMEM)] * 2,
        scratch_shapes=[pltpu.VMEM((size, 2 * size), jnp.float32)],
        name="normalise",
    )(gram, wide)


def row_products(tiles, slots, place, blocks):
    keep = (slots >= place).astype(jnp.bfloat16)
    near = jnp.take(blocks, slots, axis=0) * keep[:, None, None]
    return jnp.einsum("tab,tbn->an", tiles, near, preferred_element_type=jnp.float32)


def total(received):
    return jnp.sum(received.astype(jnp.float32), axis=0)


def local(ppmi_tiles, tile_map, sketch):
    row_id, col_id = lax.axis_index(ROW), lax.axis_index(COL)
    first_col = col_id == 0
    tiles = ppmi_tiles[0, 0]
    slots = tile_map[0, 0, 0]
    place = (row_id - 16 * col_id)[None]
    is_diag = slots == place
    diag = tiles[jnp.argmax(is_diag)]
    correction = jnp.swapaxes(jnp.triu(diag, 1), 0, 1) - jnp.tril(diag, -1)
    correction = correction * jnp.any(is_diag).astype(jnp.bfloat16)

    copies, sketch = lax.optimization_barrier((copies_of(sketch, 16), sketch))
    blocks = swap(copies, ROW)
    band_block = from_first_column(sketch)
    received = swap(column_products(tiles, slots, place, band_block, False), ROW)
    row_part = row_products(tiles, slots, place, blocks)
    row_part = row_part + jnp.dot(correction, sketch, preferred_element_type=jnp.float32)
    band = to_first_column(row_part)
    own = total(received) + jnp.where(first_col, band, 0.0)

    blocks = lax.all_gather(own, ROW, axis=0)
    gram = jnp.dot(own.T, own, precision=HIGHEST)
    both = jnp.concatenate([gram.reshape(32, 4, 128), own.reshape(32, 8, 128)], axis=1)
    both = swap(both, COL)
    piece = total(swap(copies_of(total(both[:, :4]), 16), ROW))
    both = swap(copies_of(jnp.concatenate([piece, both[0, 4:]], axis=0), 32), COL)
    gram = both[:, :4].reshape(128, 128)
    band = both[:, 4:].reshape(256, 128)
    band_block, factor = normalise(gram, band, jnp.bfloat16)

    placed = column_products(tiles, slots, place, band_block, True)
    received = total(swap(placed.reshape(4, 4, 256, 128), "x")).astype(jnp.bfloat16)
    received, blocks = lax.optimization_barrier((received, blocks))
    received = swap(received, "zl")
    blocks = lax.dot_general(
        blocks, factor, (((2,), (1,)), ((), ())), precision=HIGHEST
    ).astype(jnp.bfloat16)
    row_part = row_products(tiles, slots, place, blocks)
    row_part = row_part + jnp.dot(correction, band_block, preferred_element_type=jnp.float32)
    col_sum = total(received)
    row_part = row_part + jnp.where(first_col, col_sum, 0.0)
    rest = jnp.where(first_col, 0.0, col_sum)
    band_rows = total(swap(row_part.reshape(32, 8, 128), COL))
    stacked = jnp.concatenate([rest, band_rows], axis=0)
    gram = jnp.dot(stacked.T, stacked, precision=HIGHEST)
    piece = total(swap(gram.reshape(16, 8, 128), ROW))
    both = swap(copies_of(jnp.concatenate([piece, band_rows], axis=0), 32), COL)
    gram = swap(copies_of(total(both[:, :8]), 16), ROW).reshape(128, 128)
    own = jnp.where(first_col, both[:, 8:].reshape(256, 128), rest)
    return normalise(gram, own, jnp.float32)[0]


def solution(mesh):
    fine = Mesh(mesh.devices.reshape(4, 4, 2, 8, 2), ROW + COL)
    in_specs = (
        P(None, ROW, COL, None, None),
        P(None, ROW, COL, None),
        P(COL + ROW, None),
    )
    return jax.shard_map(
        local, mesh=fine, in_specs=in_specs, out_specs=P(COL + ROW, None), check_vma=False
    )
```

```python
import functools

import jax
import jax.numpy as jnp
from jax import lax
from jax.experimental import pallas as pl
from jax.experimental.pallas import tpu as pltpu
from jax.sharding import Mesh, PartitionSpec as P

ROW = ("zl", "x")
COL = ("zh", "y", "core")
PLANE = ("y", "core")
ACROSS = ROW + ("zh",)
HIGHEST = lax.Precision.HIGHEST
PANEL = 32


def swap(value, axes):
    return lax.all_to_all(value, axes, 0, 0, tiled=True)


def copies_of(block, count):
    return jnp.broadcast_to(block[None], (count,) + block.shape)


FAR = [[(0, 4)], [(0, 8)], [(0, 12)]]
NEAR = [[(0, 1), (4, 5)], [(0, 7), (4, 3)], [(0, 2), (4, 6)]]


def backward(pairs):
    return [(target, source) for source, target in pairs]


def from_first_column(block):
    zh, y, core = (lax.axis_index(axis) for axis in COL)
    far = sum(lax.ppermute(block, ("zh", "y"), pairs) for pairs in FAR)
    block = jnp.where((zh == 0) & (y == 0), block, far)
    near = sum(lax.ppermute(block, "y", pairs) for pairs in NEAR)
    block = jnp.where(y % 4 == 0, block, near)
    other = lax.ppermute(block, "core", [(0, 1)])
    return jnp.where(core == 0, block, other)


def to_first_column(value):
    half = value.shape[0] // 2
    core = lax.axis_index("core")
    given = lax.dynamic_slice_in_dim(value, (1 - core) * half, half)
    value = lax.dynamic_slice_in_dim(value, core * half, half)
    value = value + lax.ppermute(given, "core", [(0, 1), (1, 0)])
    value = value + sum(lax.ppermute(value, "y", backward(pairs)) for pairs in NEAR)
    value = value + sum(lax.ppermute(value, ("zh", "y"), backward(pairs)) for pairs in FAR)
    return jnp.concatenate([value, lax.ppermute(value, "core", [(1, 0)])], axis=0)


VMEM = pl.BlockSpec(memory_space=pltpu.VMEM)
SMEM = pl.BlockSpec(memory_space=pltpu.SMEM)


def column_kernel(by_x, slots_ref, place_ref, tiles_ref, band_ref, out_ref):
    band = band_ref[...]

    def one(t, carry):
        slot = slots_ref[t]
        product = lax.dot_general(
            tiles_ref[t], band, (((0,), (0,)), ((), ())), preferred_element_type=jnp.float32
        )
        where = lax.rem(slot, 4) * 4 + lax.div(slot, 4) if by_x else slot
        out_ref[where] = jnp.where(slot > place_ref[0], product, 0.0).astype(jnp.bfloat16)
        return carry

    lax.fori_loop(0, tiles_ref.shape[0], one, 0, unroll=4)


def column_products(tiles, slots, place, band_block, by_x):
    count, tile = tiles.shape[:2]
    shape = (count, tile, band_block.shape[1])
    return pl.pallas_call(
        functools.partial(column_kernel, by_x),
        out_shape=jax.ShapeDtypeStruct(shape, jnp.bfloat16),
        in_specs=[SMEM, SMEM, VMEM, VMEM],
        out_specs=VMEM,
        cost_estimate=pl.CostEstimate(
            flops=2 * count * tile * tile * shape[2], bytes_accessed=1 << 23, transcendentals=0
        ),
        name="column_products",
    )(slots, place, tiles, band_block)


def normalise_kernel(gram_ref, wide_ref, out_ref, inverse_ref, work):
    size = gram_ref.shape[0]
    work[:, :size] = gram_ref[...]
    down = lax.broadcasted_iota(jnp.int32, (size, size), 0)
    across = lax.broadcasted_iota(jnp.int32, (size, size), 1)
    work[:, size:] = (down == across).astype(jnp.float32)
    rows = lax.broadcasted_iota(jnp.int32, (PANEL, size), 0)
    for start in range(0, size, PANEL):
        left = work[start : start + PANEL, :size]
        right = work[start : start + PANEL, size:]
        lanes = [
            jnp.broadcast_to(left[:, start + j : start + j + 1], (PANEL, size))
            for j in range(PANEL)
        ]
        for k in range(PANEL):
            pivot = jnp.broadcast_to(lanes[k][k : k + 1], (PANEL, size))
            scale = lax.rsqrt(pivot)
            scale = scale * (1.5 - 0.5 * pivot * scale * scale)
            below = jnp.where(rows > k, lanes[k] * scale, 0.0)
            for j in range(k + 1, PANEL):
                lanes[j] = lanes[j] - below * jnp.broadcast_to(below[j : j + 1], (PANEL, size))
            line = left[k : k + 1] * scale[k : k + 1]
            left = jnp.where(rows == k, line, left - below * line)
            line = right[k : k + 1] * scale[k : k + 1]
            right = jnp.where(rows == k, line, right - below * line)
        both = jnp.concatenate([left, right], axis=1)
        work[start : start + PANEL, :] = both
        after = start + PANEL
        if after < size:
            update = lax.dot_general(
                left,
                both,
                (((0,), (0,)), ((), ())),
                precision=HIGHEST,
                preferred_element_type=jnp.float32,
            )
            work[after:, :] = work[after:, :] - update[after:, :]
    out = lax.dot_general(
        wide_ref[...],
        work[:, size:],
        (((1,), (1,)), ((), ())),
        precision=HIGHEST,
        preferred_element_type=jnp.float32,
    )
    out_ref[...] = out.astype(out_ref.dtype)
    inverse_ref[...] = work[:, size:]


def normalise(gram, wide, dtype):
    size = gram.shape[0]
    return pl.pallas_call(
        normalise_kernel,
        out_shape=(
            jax.ShapeDtypeStruct(wide.shape, dtype),
            jax.ShapeDtypeStruct(gram.shape, jnp.float32),
        ),
        in_specs=[pl.BlockSpec(memory_space=pltpu.VMEM)] * 2,
        out_specs=[pl.BlockSpec(memory_space=pltpu.VMEM)] * 2,
        scratch_shapes=[pltpu.VMEM((size, 2 * size), jnp.float32)],
        name="normalise",
    )(gram, wide)


def row_products(tiles, slots, place, blocks):
    keep = (slots >= place).astype(jnp.bfloat16)
    near = jnp.take(blocks, slots, axis=0) * keep[:, None, None]
    return jnp.einsum("tab,tbn->an", tiles, near, preferred_element_type=jnp.float32)


def total(received):
    return jnp.sum(received.astype(jnp.float32), axis=0)


def local(ppmi_tiles, tile_map, sketch):
    row_id, col_id = lax.axis_index(ROW), lax.axis_index(COL)
    first_col = col_id == 0
    tiles = ppmi_tiles[0, 0]
    slots = tile_map[0, 0, 0]
    place = (row_id - 16 * col_id)[None]
    is_diag = slots == place
    diag = tiles[jnp.argmax(is_diag)]
    correction = jnp.swapaxes(jnp.triu(diag, 1), 0, 1) - jnp.tril(diag, -1)
    correction = correction * jnp.any(is_diag).astype(jnp.bfloat16)

    copies, sketch = lax.optimization_barrier((copies_of(sketch, 16), sketch))
    blocks = swap(copies, ROW)
    band_block = from_first_column(sketch)
    received = swap(column_products(tiles, slots, place, band_block, False), ROW)
    row_part = row_products(tiles, slots, place, blocks)
    row_part = row_part + jnp.dot(correction, sketch, preferred_element_type=jnp.float32)
    band = to_first_column(row_part)
    own = total(received) + jnp.where(first_col, band, 0.0)

    blocks = lax.all_gather(own, ROW, axis=0)
    gram = jnp.dot(own.T, own, precision=HIGHEST)
    both = jnp.concatenate([gram.reshape(16, 8, 128), own.reshape(16, 16, 128)], axis=1)
    both = swap(both, PLANE)
    lines = both[0, 8:]
    other = lax.ppermute(lines, "zh", [(0, 1)])
    lines = jnp.where(lax.axis_index("zh") == 0, lines, other)
    piece = total(swap(copies_of(total(both[:, :8]), 32), ACROSS))
    both = swap(copies_of(jnp.concatenate([piece, lines], axis=0), 16), PLANE)
    gram = both[:, :8].reshape(128, 128)
    band = both[:, 8:].reshape(256, 128)
    band_block, factor = normalise(gram, band, jnp.bfloat16)

    placed = column_products(tiles, slots, place, band_block, True)
    received = total(swap(placed.reshape(4, 4, 256, 128), "x")).astype(jnp.bfloat16)
    received, blocks = lax.optimization_barrier((received, blocks))
    received = swap(received, "zl")
    blocks = lax.dot_general(
        blocks, factor, (((2,), (1,)), ((), ())), precision=HIGHEST
    ).astype(jnp.bfloat16)
    row_part = row_products(tiles, slots, place, blocks)
    row_part = row_part + jnp.dot(correction, band_block, preferred_element_type=jnp.float32)
    col_sum = total(received)
    row_part = row_part + jnp.where(first_col, col_sum, 0.0)
    rest = jnp.where(first_col, 0.0, col_sum)
    band_rows = total(swap(row_part.reshape(32, 8, 128), COL))
    stacked = jnp.concatenate([rest, band_rows], axis=0)
    gram = jnp.dot(stacked.T, stacked, precision=HIGHEST)
    piece = total(swap(gram.reshape(16, 8, 128), PLANE))
    piece = total(swap(copies_of(piece, 32), ACROSS))
    other = lax.ppermute(band_rows, "zh", [(1, 0)])
    both = jnp.concatenate([piece, band_rows, other], axis=0)
    both = swap(copies_of(both, 16), PLANE)
    gram = both[:, :8].reshape(128, 128)
    band = both[:, 8:].reshape(16, 2, 8, 128).swapaxes(0, 1).reshape(256, 128)
    own = jnp.where(first_col, band, rest)
    return normalise(gram, own, jnp.float32)[0]


def solution(mesh):
    fine = Mesh(mesh.devices.reshape(4, 4, 2, 8, 2), ROW + COL)
    in_specs = (
        P(None, ROW, COL, None, None),
        P(None, ROW, COL, None),
        P(COL + ROW, None),
    )
    return jax.shard_map(
        local, mesh=fine, in_specs=in_specs, out_specs=P(COL + ROW, None), check_vma=False
    )
```

```python
import functools

import jax
import jax.numpy as jnp
from jax import lax
from jax.experimental import pallas as pl
from jax.experimental.pallas import tpu as pltpu
from jax.sharding import Mesh, PartitionSpec as P

ROW = ("zl", "x")
COL = ("zh", "y", "core")
PLANE = ("y", "core")
ACROSS = ROW + ("zh",)
HIGHEST = lax.Precision.HIGHEST
PANEL = 32


def swap(value, axes):
    return lax.all_to_all(value, axes, 0, 0, tiled=True)


def copies_of(block, count):
    return jnp.broadcast_to(block[None], (count,) + block.shape)


FAR = [[(0, 4)], [(0, 8)], [(0, 12)]]
NEAR = [[(0, 1), (4, 5)], [(0, 7), (4, 3)], [(0, 2), (4, 6)]]


def backward(pairs):
    return [(target, source) for source, target in pairs]


def from_first_column(block):
    zh, y, core = (lax.axis_index(axis) for axis in COL)
    far = sum(lax.ppermute(block, ("zh", "y"), pairs) for pairs in FAR)
    block = jnp.where((zh == 0) & (y == 0), block, far)
    near = sum(lax.ppermute(block, "y", pairs) for pairs in NEAR)
    block = jnp.where(y % 4 == 0, block, near)
    other = lax.ppermute(block, "core", [(0, 1)])
    return jnp.where(core == 0, block, other)


def over_cores(value):
    half = value.shape[0] // 2
    core = lax.axis_index("core")
    given = lax.dynamic_slice_in_dim(value, (1 - core) * half, half)
    value = lax.dynamic_slice_in_dim(value, core * half, half)
    return value + lax.ppermute(given, "core", [(0, 1), (1, 0)])


def to_first_column(value):
    value = value + sum(lax.ppermute(value, "y", backward(pairs)) for pairs in NEAR)
    sent = value.astype(jnp.bfloat16)
    far = [lax.ppermute(sent, ("zh", "y"), backward(pairs)) for pairs in FAR]
    value = value + sum(part.astype(jnp.float32) for part in far)
    return jnp.concatenate([value, lax.ppermute(value, "core", [(1, 0)])], axis=0)


VMEM = pl.BlockSpec(memory_space=pltpu.VMEM)
SMEM = pl.BlockSpec(memory_space=pltpu.SMEM)


def column_kernel(by_x, slots_ref, place_ref, tiles_ref, band_ref, out_ref):
    band = band_ref[...].astype(jnp.float32).T.astype(jnp.bfloat16)
    for t in range(tiles_ref.shape[0]):
        slot = slots_ref[t]
        product = jnp.dot(band, tiles_ref[t], preferred_element_type=jnp.float32)
        product = jnp.where(slot > place_ref[0], product, 0.0).astype(jnp.bfloat16)
        where = lax.rem(slot, 4) * 4 + lax.div(slot, 4) if by_x else slot
        out_ref[where] = product.T


def column_products(tiles, slots, place, band_block, by_x):
    count, tile = tiles.shape[:2]
    shape = (count, tile, band_block.shape[1])
    return pl.pallas_call(
        functools.partial(column_kernel, by_x),
        out_shape=jax.ShapeDtypeStruct(shape, jnp.bfloat16),
        in_specs=[SMEM, SMEM, VMEM, VMEM],
        out_specs=VMEM,
        compiler_params=pltpu.CompilerParams(vmem_limit_bytes=1 << 24),
        cost_estimate=pl.CostEstimate(
            flops=2 * count * tile * tile * shape[2], bytes_accessed=1 << 23, transcendentals=0
        ),
        name="column_products",
    )(slots, place, tiles, band_block)


def normalise_kernel(both_ref, *refs):
    size = both_ref.shape[2]
    if len(refs) == 3:
        out_ref, inverse_ref, work = refs
        wide = both_ref[:, 8:].reshape(2 * size, size)
    else:
        first_ref, rest_ref, out_ref, work = refs
        halves = [both_ref[:, low : low + 8].reshape(size, size) for low in (8, 16)]
        wide = jnp.where(first_ref[0] == 0, jnp.concatenate(halves, axis=0), rest_ref[...])
    work[:, :size] = both_ref[:, :8].reshape(size, size)
    down = lax.broadcasted_iota(jnp.int32, (size, size), 0)
    across = lax.broadcasted_iota(jnp.int32, (size, size), 1)
    work[:, size:] = (down == across).astype(jnp.float32)
    rows = lax.broadcasted_iota(jnp.int32, (PANEL, size), 0)
    for start in range(0, size, PANEL):
        left = work[start : start + PANEL, :size]
        right = work[start : start + PANEL, size:]
        lanes = [
            jnp.broadcast_to(left[:, start + j : start + j + 1], (PANEL, size))
            for j in range(PANEL)
        ]
        for k in range(PANEL):
            pivot = jnp.broadcast_to(lanes[k][k : k + 1], (PANEL, size))
            scale = lax.rsqrt(pivot)
            below = jnp.where(rows > k, lanes[k] * scale, 0.0)
            for j in range(k + 1, PANEL):
                lanes[j] = lanes[j] - below * jnp.broadcast_to(below[j : j + 1], (PANEL, size))
            line = left[k : k + 1] * scale[k : k + 1]
            left = jnp.where(rows == k, line, left - below * line)
            line = right[k : k + 1] * scale[k : k + 1]
            right = jnp.where(rows == k, line, right - below * line)
        both = jnp.concatenate([left, right], axis=1)
        work[start : start + PANEL, :] = both
        after = start + PANEL
        if after < size:
            update = lax.dot_general(
                left,
                both,
                (((0,), (0,)), ((), ())),
                precision=HIGHEST,
                preferred_element_type=jnp.float32,
            )
            work[after:, :] = work[after:, :] - update[after:, :]
    out = lax.dot_general(
        wide,
        work[:, size:],
        (((1,), (1,)), ((), ())),
        precision=HIGHEST,
        preferred_element_type=jnp.float32,
    )
    out_ref[...] = out.astype(out_ref.dtype)
    if len(refs) == 3:
        inverse_ref[...] = work[:, size:]


def normalise(both, *own):
    size = both.shape[2]
    block = jax.ShapeDtypeStruct((2 * size, size), jnp.float32 if own else jnp.bfloat16)
    square = jax.ShapeDtypeStruct((size, size), jnp.float32)
    return pl.pallas_call(
        normalise_kernel,
        out_shape=block if own else (block, square),
        in_specs=[VMEM, SMEM, VMEM] if own else [VMEM],
        out_specs=VMEM if own else (VMEM, VMEM),
        scratch_shapes=[pltpu.VMEM((size, 2 * size), jnp.float32)],
        compiler_params=pltpu.CompilerParams(vmem_limit_bytes=1 << 24),
        name="normalise",
    )(both, *own)


def row_kernel(slots_ref, place_ref, tiles_ref, blocks_ref, correction_ref, band_ref, *rest):
    weight_ref, out_ref = rest if len(rest) == 2 else (None, rest[0])
    width = out_ref.shape[1]
    out = jnp.dot(correction_ref[...], band_ref[...], preferred_element_type=jnp.float32)
    for t in range(tiles_ref.shape[0]):
        slot = slots_ref[t]
        block = blocks_ref[slot]
        if weight_ref is not None:
            high = block.astype(jnp.bfloat16)
            low = (block - high.astype(jnp.float32)).astype(jnp.bfloat16)
            block = jnp.dot(
                jnp.concatenate([high, low], axis=1),
                weight_ref[...],
                preferred_element_type=jnp.float32,
            )
            block = block[:, :width] + block[:, width:]
        block = jnp.where(slot >= place_ref[0], block, 0.0).astype(jnp.bfloat16)
        out = out + jnp.dot(tiles_ref[t], block, preferred_element_type=jnp.float32)
    out_ref[...] = out


def row_products(tiles, slots, place, blocks, correction, band_block, *weight):
    count, tile = tiles.shape[:2]
    width = band_block.shape[1]
    return pl.pallas_call(
        row_kernel,
        out_shape=jax.ShapeDtypeStruct((tile, width), jnp.float32),
        in_specs=[SMEM, SMEM] + [VMEM] * (4 + len(weight)),
        out_specs=VMEM,
        compiler_params=pltpu.CompilerParams(vmem_limit_bytes=1 << 24),
        cost_estimate=pl.CostEstimate(
            flops=2 * count * tile * tile * width, bytes_accessed=1 << 23, transcendentals=0
        ),
        name="row_products",
    )(slots, place, tiles, blocks, correction, band_block, *weight)


def weight_of(factor):
    high = factor.T.astype(jnp.bfloat16)
    low = (factor.T - high.astype(jnp.float32)).astype(jnp.bfloat16)
    return jnp.block([[high, low], [high, jnp.zeros_like(high)]])


def total(received):
    return jnp.sum(received.astype(jnp.float32), axis=0)


def local(ppmi_tiles, tile_map, sketch):
    row_id, col_id = lax.axis_index(ROW), lax.axis_index(COL)
    first_col = col_id == 0
    tiles = ppmi_tiles[0, 0]
    slots = tile_map[0, 0, 0]
    place = (row_id - 16 * col_id)[None]
    is_diag = slots == place
    diag = tiles[jnp.argmax(is_diag)]
    correction = jnp.swapaxes(jnp.triu(diag, 1), 0, 1) - jnp.tril(diag, -1)
    correction = correction * jnp.any(is_diag).astype(jnp.bfloat16)

    copies, sketch = lax.optimization_barrier((copies_of(sketch, 16), sketch))
    blocks = swap(copies, ROW)
    band_block = from_first_column(sketch)
    received = swap(column_products(tiles, slots, place, band_block, False), ROW)
    row_part = row_products(tiles, slots, place, blocks, correction, sketch)
    band = to_first_column(over_cores(row_part))
    own = total(received) + jnp.where(first_col, band, 0.0)

    blocks = lax.all_gather(own, ROW, axis=0)
    gram = jnp.dot(own.T, own, precision=HIGHEST)
    both = jnp.concatenate([gram.reshape(16, 8, 128), own.reshape(16, 16, 128)], axis=1)
    both = swap(both, PLANE)
    lines = both[0, 8:]
    other = lax.ppermute(lines, "zh", [(0, 1)])
    lines = jnp.where(lax.axis_index("zh") == 0, lines, other)
    piece = total(swap(copies_of(total(both[:, :8]), 32), ACROSS))
    both = swap(copies_of(jnp.concatenate([piece, lines], axis=0), 16), PLANE)
    band_block, factor = normalise(both)

    placed = column_products(tiles, slots, place, band_block, True)
    received = total(swap(placed.reshape(4, 4, 256, 128), "x")).astype(jnp.bfloat16)
    received, blocks = lax.optimization_barrier((received, blocks))
    received = swap(received, "zl")
    row_part = row_products(
        tiles, slots, place, blocks, correction, band_block, weight_of(factor)
    )
    col_sum = total(received)
    row_part = row_part + jnp.where(first_col, col_sum, 0.0)
    rest = jnp.where(first_col, 0.0, col_sum)
    band_rows = total(swap(row_part.reshape(32, 8, 128), COL))
    stacked = jnp.concatenate([rest, band_rows], axis=0)
    gram = jnp.dot(stacked.T, stacked, precision=HIGHEST)
    piece = total(swap(gram.reshape(16, 8, 128), PLANE))
    piece = total(swap(copies_of(piece, 32), ACROSS))
    other = lax.ppermute(band_rows, "zh", [(1, 0)])
    both = jnp.concatenate([piece, band_rows, other], axis=0)
    both = swap(copies_of(both, 16), PLANE)
    return normalise(both, col_id[None], rest)


def solution(mesh):
    fine = Mesh(mesh.devices.reshape(4, 4, 2, 8, 2), ROW + COL)
    in_specs = (
        P(None, ROW, COL, None, None),
        P(None, ROW, COL, None),
        P(COL + ROW, None),
    )
    return jax.shard_map(
        local, mesh=fine, in_specs=in_specs, out_specs=P(COL + ROW, None), check_vma=False
    )
```

```python
import functools

import jax
import jax.numpy as jnp
from jax import lax
from jax.experimental import pallas as pl
from jax.experimental.pallas import tpu as pltpu
from jax.sharding import Mesh, PartitionSpec as P

ROW = ("zl", "x")
COL = ("zh", "y", "core")
PLANE = ("y", "core")
ACROSS = ROW + ("zh",)
HIGHEST = lax.Precision.HIGHEST
PANEL = 32


def swap(value, axes):
    return lax.all_to_all(value, axes, 0, 0, tiled=True)


def copies_of(block, count):
    return jnp.broadcast_to(block[None], (count,) + block.shape)


FAR = [[(0, 4)], [(0, 8)], [(0, 12)]]
NEAR = [[(0, 1), (4, 5)], [(0, 7), (4, 3)], [(0, 2), (4, 6)]]


def backward(pairs):
    return [(target, source) for source, target in pairs]


def from_first_column(block):
    zh, y, core = (lax.axis_index(axis) for axis in COL)
    far = sum(lax.ppermute(block, ("zh", "y"), pairs) for pairs in FAR)
    block = jnp.where((zh == 0) & (y == 0), block, far)
    near = sum(lax.ppermute(block, "y", pairs) for pairs in NEAR)
    block = jnp.where(y % 4 == 0, block, near)
    other = lax.ppermute(block, "core", [(0, 1)])
    return jnp.where(core == 0, block, other)


def over_cores(value):
    half = value.shape[0] // 2
    core = lax.axis_index("core")
    given = lax.dynamic_slice_in_dim(value, (1 - core) * half, half)
    value = lax.dynamic_slice_in_dim(value, core * half, half)
    return value + lax.ppermute(given, "core", [(0, 1), (1, 0)])


def to_first_column(value):
    value = value + sum(lax.ppermute(value, "y", backward(pairs)) for pairs in NEAR)
    value = value + sum(lax.ppermute(value, ("zh", "y"), backward(pairs)) for pairs in FAR)
    return jnp.concatenate([value, lax.ppermute(value, "core", [(1, 0)])], axis=0)


VMEM = pl.BlockSpec(memory_space=pltpu.VMEM)
SMEM = pl.BlockSpec(memory_space=pltpu.SMEM)


def column_kernel(by_x, slots_ref, place_ref, tiles_ref, band_ref, out_ref):
    band = band_ref[...].astype(jnp.float32).T.astype(jnp.bfloat16)
    for t in range(tiles_ref.shape[0]):
        slot = slots_ref[t]
        product = jnp.dot(band, tiles_ref[t], preferred_element_type=jnp.float32)
        product = jnp.where(slot > place_ref[0], product, 0.0).astype(jnp.bfloat16)
        where = lax.rem(slot, 4) * 4 + lax.div(slot, 4) if by_x else slot
        out_ref[where] = product.T


def column_products(tiles, slots, place, band_block, by_x):
    count, tile = tiles.shape[:2]
    shape = (count, tile, band_block.shape[1])
    return pl.pallas_call(
        functools.partial(column_kernel, by_x),
        out_shape=jax.ShapeDtypeStruct(shape, jnp.bfloat16),
        in_specs=[SMEM, SMEM, VMEM, VMEM],
        out_specs=VMEM,
        compiler_params=pltpu.CompilerParams(vmem_limit_bytes=1 << 24),
        cost_estimate=pl.CostEstimate(
            flops=2 * count * tile * tile * shape[2], bytes_accessed=1 << 23, transcendentals=0
        ),
        name="column_products",
    )(slots, place, tiles, band_block)


def normalise_kernel(both_ref, *refs):
    size = both_ref.shape[2]
    if len(refs) == 3:
        out_ref, inverse_ref, work = refs
        wide = both_ref[:, 8:].reshape(2 * size, size)
    else:
        first_ref, rest_ref, out_ref, work = refs
        halves = [both_ref[:, low : low + 8].reshape(size, size) for low in (8, 16)]
        wide = jnp.where(first_ref[0] == 0, jnp.concatenate(halves, axis=0), rest_ref[...])
    work[:, :size] = both_ref[:, :8].reshape(size, size)
    down = lax.broadcasted_iota(jnp.int32, (size, size), 0)
    across = lax.broadcasted_iota(jnp.int32, (size, size), 1)
    work[:, size:] = (down == across).astype(jnp.float32)
    rows = lax.broadcasted_iota(jnp.int32, (PANEL, size), 0)
    for start in range(0, size, PANEL):
        left = work[start : start + PANEL, :size]
        right = work[start : start + PANEL, size:]
        lanes = [
            jnp.broadcast_to(left[:, start + j : start + j + 1], (PANEL, size))
            for j in range(PANEL)
        ]
        for k in range(PANEL):
            pivot = jnp.broadcast_to(lanes[k][k : k + 1], (PANEL, size))
            scale = lax.rsqrt(pivot)
            below = jnp.where(rows > k, lanes[k] * scale, 0.0)
            for j in range(k + 1, PANEL):
                lanes[j] = lanes[j] - below * jnp.broadcast_to(below[j : j + 1], (PANEL, size))
            line = left[k : k + 1] * scale[k : k + 1]
            left = jnp.where(rows == k, line, left - below * line)
            line = right[k : k + 1] * scale[k : k + 1]
            right = jnp.where(rows == k, line, right - below * line)
        both = jnp.concatenate([left, right], axis=1)
        work[start : start + PANEL, :] = both
        after = start + PANEL
        if after < size:
            update = lax.dot_general(
                left,
                both,
                (((0,), (0,)), ((), ())),
                precision=HIGHEST,
                preferred_element_type=jnp.float32,
            )
            work[after:, :] = work[after:, :] - update[after:, :]
    out = lax.dot_general(
        wide,
        work[:, size:],
        (((1,), (1,)), ((), ())),
        precision=HIGHEST,
        preferred_element_type=jnp.float32,
    )
    out_ref[...] = out.astype(out_ref.dtype)
    if len(refs) == 3:
        inverse_ref[...] = work[:, size:]


def normalise(both, *own):
    size = both.shape[2]
    block = jax.ShapeDtypeStruct((2 * size, size), jnp.float32 if own else jnp.bfloat16)
    square = jax.ShapeDtypeStruct((size, size), jnp.float32)
    return pl.pallas_call(
        normalise_kernel,
        out_shape=block if own else (block, square),
        in_specs=[VMEM, SMEM, VMEM] if own else [VMEM],
        out_specs=VMEM if own else (VMEM, VMEM),
        scratch_shapes=[pltpu.VMEM((size, 2 * size), jnp.float32)],
        compiler_params=pltpu.CompilerParams(vmem_limit_bytes=1 << 24),
        name="normalise",
    )(both, *own)


def row_kernel(slots_ref, place_ref, tiles_ref, blocks_ref, correction_ref, band_ref, *rest):
    weight_ref, out_ref = rest if len(rest) == 2 else (None, rest[0])
    width = out_ref.shape[1]
    out = jnp.dot(correction_ref[...], band_ref[...], preferred_element_type=jnp.float32)
    for t in range(tiles_ref.shape[0]):
        slot = slots_ref[t]
        block = blocks_ref[slot]
        if weight_ref is not None:
            high = block.astype(jnp.bfloat16)
            low = (block - high.astype(jnp.float32)).astype(jnp.bfloat16)
            block = jnp.dot(
                jnp.concatenate([high, low], axis=1),
                weight_ref[...],
                preferred_element_type=jnp.float32,
            )
            block = block[:, :width] + block[:, width:]
        block = jnp.where(slot >= place_ref[0], block, 0.0).astype(jnp.bfloat16)
        out = out + jnp.dot(tiles_ref[t], block, preferred_element_type=jnp.float32)
    out_ref[...] = out


def row_products(tiles, slots, place, blocks, correction, band_block, *weight):
    count, tile = tiles.shape[:2]
    width = band_block.shape[1]
    return pl.pallas_call(
        row_kernel,
        out_shape=jax.ShapeDtypeStruct((tile, width), jnp.float32),
        in_specs=[SMEM, SMEM] + [VMEM] * (4 + len(weight)),
        out_specs=VMEM,
        compiler_params=pltpu.CompilerParams(vmem_limit_bytes=1 << 24),
        cost_estimate=pl.CostEstimate(
            flops=2 * count * tile * tile * width, bytes_accessed=1 << 23, transcendentals=0
        ),
        name="row_products",
    )(slots, place, tiles, blocks, correction, band_block, *weight)


def weight_of(factor):
    high = factor.T.astype(jnp.bfloat16)
    low = (factor.T - high.astype(jnp.float32)).astype(jnp.bfloat16)
    return jnp.block([[high, low], [high, jnp.zeros_like(high)]])


def total(received):
    return jnp.sum(received.astype(jnp.float32), axis=0)


def local(ppmi_tiles, tile_map, sketch):
    row_id, col_id = lax.axis_index(ROW), lax.axis_index(COL)
    first_col = col_id == 0
    tiles = ppmi_tiles[0, 0]
    slots = tile_map[0, 0, 0]
    place = (row_id - 16 * col_id)[None]
    is_diag = slots == place
    diag = tiles[jnp.argmax(is_diag)]
    correction = jnp.swapaxes(jnp.triu(diag, 1), 0, 1) - jnp.tril(diag, -1)
    correction = correction * jnp.any(is_diag).astype(jnp.bfloat16)

    copies, sketch = lax.optimization_barrier((copies_of(sketch, 16), sketch))
    blocks = swap(copies, ROW)
    band_block = from_first_column(sketch)
    received = swap(column_products(tiles, slots, place, band_block, False), ROW)
    row_part = row_products(tiles, slots, place, blocks, correction, sketch)
    band = to_first_column(over_cores(row_part))
    own = total(received) + jnp.where(first_col, band, 0.0)

    blocks = lax.all_gather(own, ROW, axis=0)
    gram = jnp.dot(own.T, own, precision=HIGHEST)
    both = jnp.concatenate([gram.reshape(16, 8, 128), own.reshape(16, 16, 128)], axis=1)
    both = swap(both, PLANE)
    lines = both[0, 8:]
    other = lax.ppermute(lines, "zh", [(0, 1)])
    lines = jnp.where(lax.axis_index("zh") == 0, lines, other)
    piece = total(swap(copies_of(total(both[:, :8]), 32), ACROSS))
    both = swap(copies_of(jnp.concatenate([piece, lines], axis=0), 16), PLANE)
    band_block, factor = normalise(both)

    placed = column_products(tiles, slots, place, band_block, True)
    received = total(swap(placed.reshape(4, 4, 256, 128), "x")).astype(jnp.bfloat16)
    received = swap(received, "zl")
    row_part = row_products(
        tiles, slots, place, blocks, correction, band_block, weight_of(factor)
    )
    col_sum = total(received)
    row_part = row_part + jnp.where(first_col, col_sum, 0.0)
    rest = jnp.where(first_col, 0.0, col_sum)
    band_rows = total(swap(row_part.reshape(32, 8, 128), COL))
    stacked = jnp.concatenate([rest, band_rows], axis=0)
    gram = jnp.dot(stacked.T, stacked, precision=HIGHEST)
    piece = total(swap(gram.reshape(16, 8, 128), PLANE))
    piece = total(swap(copies_of(piece, 32), ACROSS))
    other = lax.ppermute(band_rows, "zh", [(1, 0)])
    both = jnp.concatenate([piece, band_rows, other], axis=0)
    both = swap(copies_of(both, 16), PLANE)
    return normalise(both, col_id[None], rest)


def solution(mesh):
    fine = Mesh(mesh.devices.reshape(4, 4, 2, 8, 2), ROW + COL)
    in_specs = (
        P(None, ROW, COL, None, None),
        P(None, ROW, COL, None),
        P(COL + ROW, None),
    )
    return jax.shard_map(
        local, mesh=fine, in_specs=in_specs, out_specs=P(COL + ROW, None), check_vma=False
    )
```

```python
import functools

import jax
import jax.numpy as jnp
from jax import lax
from jax.experimental import pallas as pl
from jax.experimental.pallas import tpu as pltpu
from jax.sharding import Mesh, PartitionSpec as P

ROW = ("zl", "x")
COL = ("zh", "y", "core")
PLANE = ("y", "core")
ACROSS = ROW + ("zh",)
HIGHEST = lax.Precision.HIGHEST
PANEL = 32


def swap(value, axes):
    return lax.all_to_all(value, axes, 0, 0, tiled=True)


def copies_of(block, count):
    return jnp.broadcast_to(block[None], (count,) + block.shape)


FAR = [[(0, 4)], [(0, 10)], [(0, 14)]]
NEAR = [
    [(0, 1), (4, 5), (10, 11), (14, 15)],
    [(0, 7), (4, 3), (10, 9), (14, 13)],
    [(0, 2), (4, 6), (10, 12), (14, 8)],
]


def backward(pairs):
    return [(target, source) for source, target in pairs]


def from_first_column(block):
    zh, y, core = (lax.axis_index(axis) for axis in COL)
    far = sum(lax.ppermute(block, ("zh", "y"), pairs) for pairs in FAR)
    block = jnp.where((zh == 0) & (y == 0), block, far)
    near = sum(lax.ppermute(block, ("zh", "y"), pairs) for pairs in NEAR)
    block = jnp.where(y % 4 == 2 * zh, block, near)
    other = lax.ppermute(block, "core", [(0, 1)])
    return jnp.where(core == 0, block, other)


def over_cores(value):
    half = value.shape[0] // 2
    core = lax.axis_index("core")
    given = lax.dynamic_slice_in_dim(value, (1 - core) * half, half)
    value = lax.dynamic_slice_in_dim(value, core * half, half)
    return value + lax.ppermute(given, "core", [(0, 1), (1, 0)])


def to_first_column(value):
    value = value + sum(lax.ppermute(value, ("zh", "y"), backward(pairs)) for pairs in NEAR)
    sent = value.astype(jnp.bfloat16)
    far = lax.ppermute(value, ("zh", "y"), backward(FAR[0]))
    for pairs in FAR[1:]:
        far = far + lax.ppermute(sent, ("zh", "y"), backward(pairs)).astype(jnp.float32)
    value = value + far
    return jnp.concatenate([value, lax.ppermute(value, "core", [(1, 0)])], axis=0)


VMEM = pl.BlockSpec(memory_space=pltpu.VMEM)
SMEM = pl.BlockSpec(memory_space=pltpu.SMEM)


def column_kernel(by_x, slots_ref, place_ref, tiles_ref, band_ref, out_ref):
    band = band_ref[...].astype(jnp.float32).T.astype(jnp.bfloat16)
    for t in range(tiles_ref.shape[0]):
        slot = slots_ref[t]
        product = jnp.dot(band, tiles_ref[t], preferred_element_type=jnp.float32)
        product = jnp.where(slot > place_ref[0], product, 0.0).astype(jnp.bfloat16)
        where = lax.rem(slot, 4) * 4 + lax.div(slot, 4) if by_x else slot
        out_ref[where] = product.T


def column_products(tiles, slots, place, band_block, by_x):
    count, tile = tiles.shape[:2]
    shape = (count, tile, band_block.shape[1])
    return pl.pallas_call(
        functools.partial(column_kernel, by_x),
        out_shape=jax.ShapeDtypeStruct(shape, jnp.bfloat16),
        in_specs=[SMEM, SMEM, VMEM, VMEM],
        out_specs=VMEM,
        compiler_params=pltpu.CompilerParams(vmem_limit_bytes=1 << 24),
        cost_estimate=pl.CostEstimate(
            flops=2 * count * tile * tile * shape[2], bytes_accessed=1 << 23, transcendentals=0
        ),
        name="column_products",
    )(slots, place, tiles, band_block)


def normalise_kernel(both_ref, *refs):
    size = both_ref.shape[2]
    if len(refs) == 3:
        out_ref, inverse_ref, work = refs
        wide = both_ref[:, 8:].reshape(2 * size, size)
    else:
        first_ref, rest_ref, out_ref, work = refs
        halves = [both_ref[:, low : low + 8].reshape(size, size) for low in (8, 16)]
        wide = jnp.where(first_ref[0] == 0, jnp.concatenate(halves, axis=0), rest_ref[...])
    work[:, :size] = both_ref[:, :8].reshape(size, size)
    down = lax.broadcasted_iota(jnp.int32, (size, size), 0)
    across = lax.broadcasted_iota(jnp.int32, (size, size), 1)
    work[:, size:] = (down == across).astype(jnp.float32)
    rows = lax.broadcasted_iota(jnp.int32, (PANEL, size), 0)
    for start in range(0, size, PANEL):
        left = work[start : start + PANEL, :size]
        right = work[start : start + PANEL, size:]
        lanes = [
            jnp.broadcast_to(left[:, start + j : start + j + 1], (PANEL, size))
            for j in range(PANEL)
        ]
        for k in range(PANEL):
            pivot = jnp.broadcast_to(lanes[k][k : k + 1], (PANEL, size))
            scale = lax.rsqrt(pivot)
            below = jnp.where(rows > k, lanes[k] * scale, 0.0)
            for j in range(k + 1, PANEL):
                lanes[j] = lanes[j] - below * jnp.broadcast_to(below[j : j + 1], (PANEL, size))
            line = left[k : k + 1] * scale[k : k + 1]
            left = jnp.where(rows == k, line, left - below * line)
            line = right[k : k + 1] * scale[k : k + 1]
            right = jnp.where(rows == k, line, right - below * line)
        both = jnp.concatenate([left, right], axis=1)
        work[start : start + PANEL, :] = both
        after = start + PANEL
        if after < size:
            update = lax.dot_general(
                left,
                both,
                (((0,), (0,)), ((), ())),
                precision=HIGHEST,
                preferred_element_type=jnp.float32,
            )
            work[after:, :] = work[after:, :] - update[after:, :]
    out = lax.dot_general(
        wide,
        work[:, size:],
        (((1,), (1,)), ((), ())),
        precision=HIGHEST,
        preferred_element_type=jnp.float32,
    )
    out_ref[...] = out.astype(out_ref.dtype)
    if len(refs) == 3:
        inverse_ref[...] = work[:, size:]


def normalise(both, *own):
    size = both.shape[2]
    block = jax.ShapeDtypeStruct((2 * size, size), jnp.float32 if own else jnp.bfloat16)
    square = jax.ShapeDtypeStruct((size, size), jnp.float32)
    return pl.pallas_call(
        normalise_kernel,
        out_shape=block if own else (block, square),
        in_specs=[VMEM, SMEM, VMEM] if own else [VMEM],
        out_specs=VMEM if own else (VMEM, VMEM),
        scratch_shapes=[pltpu.VMEM((size, 2 * size), jnp.float32)],
        compiler_params=pltpu.CompilerParams(vmem_limit_bytes=1 << 24),
        name="normalise",
    )(both, *own)


def row_kernel(slots_ref, place_ref, tiles_ref, blocks_ref, correction_ref, band_ref, *rest):
    weight_ref, out_ref = rest if len(rest) == 2 else (None, rest[0])
    width = out_ref.shape[1]
    out = jnp.dot(correction_ref[...], band_ref[...], preferred_element_type=jnp.float32)
    for t in range(tiles_ref.shape[0]):
        slot = slots_ref[t]
        block = blocks_ref[slot]
        if weight_ref is not None:
            high = block.astype(jnp.bfloat16)
            low = (block - high.astype(jnp.float32)).astype(jnp.bfloat16)
            block = jnp.dot(
                jnp.concatenate([high, low], axis=1),
                weight_ref[...],
                preferred_element_type=jnp.float32,
            )
            block = block[:, :width] + block[:, width:]
        block = jnp.where(slot >= place_ref[0], block, 0.0).astype(jnp.bfloat16)
        out = out + jnp.dot(tiles_ref[t], block, preferred_element_type=jnp.float32)
    out_ref[...] = out


def row_products(tiles, slots, place, blocks, correction, band_block, *weight):
    count, tile = tiles.shape[:2]
    width = band_block.shape[1]
    return pl.pallas_call(
        row_kernel,
        out_shape=jax.ShapeDtypeStruct((tile, width), jnp.float32),
        in_specs=[SMEM, SMEM] + [VMEM] * (4 + len(weight)),
        out_specs=VMEM,
        compiler_params=pltpu.CompilerParams(vmem_limit_bytes=1 << 24),
        cost_estimate=pl.CostEstimate(
            flops=2 * count * tile * tile * width, bytes_accessed=1 << 23, transcendentals=0
        ),
        name="row_products",
    )(slots, place, tiles, blocks, correction, band_block, *weight)


def weight_of(factor):
    high = factor.T.astype(jnp.bfloat16)
    low = (factor.T - high.astype(jnp.float32)).astype(jnp.bfloat16)
    return jnp.block([[high, low], [high, jnp.zeros_like(high)]])


def total(received):
    return jnp.sum(received.astype(jnp.float32), axis=0)


def local(ppmi_tiles, tile_map, sketch):
    row_id, col_id = lax.axis_index(ROW), lax.axis_index(COL)
    first_col = col_id == 0
    tiles = ppmi_tiles[0, 0]
    slots = tile_map[0, 0, 0]
    place = (row_id - 16 * col_id)[None]
    is_diag = slots == place
    diag = tiles[jnp.argmax(is_diag)]
    correction = jnp.swapaxes(jnp.triu(diag, 1), 0, 1) - jnp.tril(diag, -1)
    correction = correction * jnp.any(is_diag).astype(jnp.bfloat16)

    copies, sketch = lax.optimization_barrier((copies_of(sketch, 16), sketch))
    blocks = swap(copies, ROW)
    band_block = from_first_column(sketch)
    received = swap(column_products(tiles, slots, place, band_block, False), ROW)
    row_part = row_products(tiles, slots, place, blocks, correction, sketch)
    band = to_first_column(over_cores(row_part))
    own = total(received) + jnp.where(first_col, band, 0.0)

    blocks = lax.all_gather(own, ROW, axis=0)
    gram = jnp.dot(own.T, own, precision=HIGHEST)
    both = jnp.concatenate([gram.reshape(16, 8, 128), own.reshape(16, 16, 128)], axis=1)
    both = swap(both, PLANE)
    lines = both[0, 8:]
    other = lax.ppermute(lines, "zh", [(0, 1)])
    lines = jnp.where(lax.axis_index("zh") == 0, lines, other)
    piece = total(swap(copies_of(total(both[:, :8]), 32), ACROSS))
    both = swap(copies_of(jnp.concatenate([piece, lines], axis=0), 16), PLANE)
    band_block, factor = normalise(both)

    placed = column_products(tiles, slots, place, band_block, True)
    received = total(swap(placed.reshape(4, 4, 256, 128), "x")).astype(jnp.bfloat16)
    received = swap(received, "zl")
    row_part = row_products(
        tiles, slots, place, blocks, correction, band_block, weight_of(factor)
    )
    col_sum = total(received)
    row_part = row_part + jnp.where(first_col, col_sum, 0.0)
    rest = jnp.where(first_col, 0.0, col_sum)
    band_rows = total(swap(row_part.reshape(32, 8, 128), COL))
    stacked = jnp.concatenate([rest, band_rows], axis=0)
    gram = jnp.dot(stacked.T, stacked, precision=HIGHEST)
    piece = total(swap(gram.reshape(16, 8, 128), PLANE))
    piece = total(swap(copies_of(piece, 32), ACROSS))
    other = lax.ppermute(band_rows, "zh", [(1, 0)])
    both = jnp.concatenate([piece, band_rows, other], axis=0)
    both = swap(copies_of(both, 16), PLANE)
    return normalise(both, col_id[None], rest)


def solution(mesh):
    fine = Mesh(mesh.devices.reshape(4, 4, 2, 8, 2), ROW + COL)
    in_specs = (
        P(None, ROW, COL, None, None),
        P(None, ROW, COL, None),
        P(COL + ROW, None),
    )
    return jax.shard_map(
        local, mesh=fine, in_specs=in_specs, out_specs=P(COL + ROW, None), check_vma=False
    )
```

```python
import functools

import jax
import jax.numpy as jnp
from jax import lax
from jax.experimental import pallas as pl
from jax.experimental.pallas import tpu as pltpu
from jax.sharding import Mesh, PartitionSpec as P

ROW = ("zl", "x")
COL = ("zh", "y", "core")
PLANE = ("y", "core")
ACROSS = ROW + ("zh",)
HIGHEST = lax.Precision.HIGHEST
PANEL = 32


def swap(value, axes):
    return lax.all_to_all(value, axes, 0, 0, tiled=True)


def copies_of(block, count):
    return jnp.broadcast_to(block[None], (count,) + block.shape)


FAR = [[(0, 4)], [(0, 10)], [(0, 14)]]
NEAR = [
    [(0, 1), (4, 5), (10, 11), (14, 15)],
    [(0, 7), (4, 3), (10, 9), (14, 13)],
    [(0, 2), (4, 6), (10, 12), (14, 8)],
]


def backward(pairs):
    return [(target, source) for source, target in pairs]


def from_first_column(block):
    zh, y, core = (lax.axis_index(axis) for axis in COL)
    far = sum(lax.ppermute(block, ("zh", "y"), pairs) for pairs in FAR)
    block = jnp.where((zh == 0) & (y == 0), block, far)
    near = sum(lax.ppermute(block, ("zh", "y"), pairs) for pairs in NEAR)
    block = jnp.where(y % 4 == 2 * zh, block, near)
    other = lax.ppermute(block, "core", [(0, 1)])
    return jnp.where(core == 0, block, other)


def over_cores(value):
    half = value.shape[0] // 2
    core = lax.axis_index("core")
    given = lax.dynamic_slice_in_dim(value, (1 - core) * half, half)
    value = lax.dynamic_slice_in_dim(value, core * half, half)
    return value + lax.ppermute(given, "core", [(0, 1), (1, 0)])


def to_first_column(value):
    value = value + sum(lax.ppermute(value, ("zh", "y"), backward(pairs)) for pairs in NEAR)
    sent = value.astype(jnp.bfloat16)
    far = lax.ppermute(value, ("zh", "y"), backward(FAR[0]))
    for pairs in FAR[1:]:
        far = far + lax.ppermute(sent, ("zh", "y"), backward(pairs)).astype(jnp.float32)
    value = value + far
    return jnp.concatenate([value, lax.ppermute(value, "core", [(1, 0)])], axis=0)


VMEM = pl.BlockSpec(memory_space=pltpu.VMEM)
SMEM = pl.BlockSpec(memory_space=pltpu.SMEM)


def column_kernel(by_x, slots_ref, place_ref, tiles_ref, band_ref, out_ref):
    band = band_ref[...].astype(jnp.float32).T.astype(jnp.bfloat16)
    for t in range(tiles_ref.shape[0]):
        slot = slots_ref[t]
        product = jnp.dot(band, tiles_ref[t], preferred_element_type=jnp.float32)
        product = jnp.where(slot > place_ref[0], product, 0.0).astype(jnp.bfloat16)
        where = lax.rem(slot, 4) * 4 + lax.div(slot, 4) if by_x else slot
        out_ref[where] = product.T


def column_products(tiles, slots, place, band_block, by_x):
    count, tile = tiles.shape[:2]
    shape = (count, tile, band_block.shape[1])
    return pl.pallas_call(
        functools.partial(column_kernel, by_x),
        out_shape=jax.ShapeDtypeStruct(shape, jnp.bfloat16),
        in_specs=[SMEM, SMEM, VMEM, VMEM],
        out_specs=VMEM,
        compiler_params=pltpu.CompilerParams(vmem_limit_bytes=1 << 24),
        cost_estimate=pl.CostEstimate(
            flops=2 * count * tile * tile * shape[2], bytes_accessed=1 << 23, transcendentals=0
        ),
        name="column_products",
    )(slots, place, tiles, band_block)


def normalise_kernel(both_ref, *refs):
    size = both_ref.shape[2]
    if len(refs) == 3:
        out_ref, inverse_ref, work = refs
        wide = both_ref[:, 8:].reshape(2 * size, size)
    else:
        first_ref, rest_ref, out_ref, work = refs
        halves = [both_ref[:, low : low + 8].reshape(size, size) for low in (8, 16)]
        wide = jnp.where(first_ref[0] == 0, jnp.concatenate(halves, axis=0), rest_ref[...])
    work[:, :size] = both_ref[:, :8].reshape(size, size)
    down = lax.broadcasted_iota(jnp.int32, (size, size), 0)
    across = lax.broadcasted_iota(jnp.int32, (size, size), 1)
    work[:, size:] = (down == across).astype(jnp.float32)
    rows = lax.broadcasted_iota(jnp.int32, (PANEL, size), 0)
    for start in range(0, size, PANEL):
        left = work[start : start + PANEL, :size]
        right = work[start : start + PANEL, size:]
        lanes = [
            jnp.broadcast_to(left[:, start + j : start + j + 1], (PANEL, size))
            for j in range(PANEL)
        ]
        for k in range(PANEL):
            pivot = jnp.broadcast_to(lanes[k][k : k + 1], (PANEL, size))
            scale = lax.rsqrt(pivot)
            below = jnp.where(rows > k, lanes[k] * scale, 0.0)
            for j in range(k + 1, PANEL):
                lanes[j] = lanes[j] - below * jnp.broadcast_to(below[j : j + 1], (PANEL, size))
            line = left[k : k + 1] * scale[k : k + 1]
            left = jnp.where(rows == k, line, left - below * line)
            line = right[k : k + 1] * scale[k : k + 1]
            right = jnp.where(rows == k, line, right - below * line)
        both = jnp.concatenate([left, right], axis=1)
        work[start : start + PANEL, :] = both
        after = start + PANEL
        if after < size:
            update = lax.dot_general(
                left,
                both,
                (((0,), (0,)), ((), ())),
                precision=HIGHEST,
                preferred_element_type=jnp.float32,
            )
            work[after:, :] = work[after:, :] - update[after:, :]
    out = lax.dot_general(
        wide,
        work[:, size:],
        (((1,), (1,)), ((), ())),
        precision=HIGHEST,
        preferred_element_type=jnp.float32,
    )
    out_ref[...] = out.astype(out_ref.dtype)
    if len(refs) == 3:
        inverse_ref[...] = work[:, size:]


def normalise(both, *own):
    size = both.shape[2]
    block = jax.ShapeDtypeStruct((2 * size, size), jnp.float32 if own else jnp.bfloat16)
    square = jax.ShapeDtypeStruct((size, size), jnp.float32)
    return pl.pallas_call(
        normalise_kernel,
        out_shape=block if own else (block, square),
        in_specs=[VMEM, SMEM, VMEM] if own else [VMEM],
        out_specs=VMEM if own else (VMEM, VMEM),
        scratch_shapes=[pltpu.VMEM((size, 2 * size), jnp.float32)],
        compiler_params=pltpu.CompilerParams(vmem_limit_bytes=1 << 24),
        name="normalise",
    )(both, *own)


def row_kernel(slots_ref, place_ref, tiles_ref, blocks_ref, correction_ref, band_ref, *rest):
    weight_ref, out_ref = rest if len(rest) == 2 else (None, rest[0])
    width = out_ref.shape[1]
    out = jnp.dot(correction_ref[...], band_ref[...], preferred_element_type=jnp.float32)
    for t in range(tiles_ref.shape[0]):
        slot = slots_ref[t]
        block = blocks_ref[slot]
        if weight_ref is not None:
            high = block.astype(jnp.bfloat16)
            low = (block - high.astype(jnp.float32)).astype(jnp.bfloat16)
            block = jnp.dot(
                jnp.concatenate([high, low], axis=1),
                weight_ref[...],
                preferred_element_type=jnp.float32,
            )
            block = block[:, :width] + block[:, width:]
        block = jnp.where(slot >= place_ref[0], block, 0.0).astype(jnp.bfloat16)
        out = out + jnp.dot(tiles_ref[t], block, preferred_element_type=jnp.float32)
    out_ref[...] = out


def row_products(tiles, slots, place, blocks, correction, band_block, *weight):
    count, tile = tiles.shape[:2]
    width = band_block.shape[1]
    return pl.pallas_call(
        row_kernel,
        out_shape=jax.ShapeDtypeStruct((tile, width), jnp.float32),
        in_specs=[SMEM, SMEM] + [VMEM] * (4 + len(weight)),
        out_specs=VMEM,
        compiler_params=pltpu.CompilerParams(vmem_limit_bytes=1 << 24),
        cost_estimate=pl.CostEstimate(
            flops=2 * count * tile * tile * width, bytes_accessed=1 << 23, transcendentals=0
        ),
        name="row_products",
    )(slots, place, tiles, blocks, correction, band_block, *weight)


def weight_of(factor):
    high = factor.T.astype(jnp.bfloat16)
    low = (factor.T - high.astype(jnp.float32)).astype(jnp.bfloat16)
    return jnp.block([[high, low], [high, jnp.zeros_like(high)]])


def total_of_four(received):
    first, second, third, fourth = (received[i].astype(jnp.float32) for i in range(4))
    return (first + second) + (third + fourth)


def total(received):
    return jnp.sum(received.astype(jnp.float32), axis=0)


def local(ppmi_tiles, tile_map, sketch):
    row_id, col_id = lax.axis_index(ROW), lax.axis_index(COL)
    first_col = col_id == 0
    tiles = ppmi_tiles[0, 0]
    slots = tile_map[0, 0, 0]
    place = (row_id - 16 * col_id)[None]
    is_diag = slots == place
    diag = tiles[jnp.argmax(is_diag)]
    correction = jnp.swapaxes(jnp.triu(diag, 1), 0, 1) - jnp.tril(diag, -1)
    correction = correction * jnp.any(is_diag).astype(jnp.bfloat16)

    copies, sketch = lax.optimization_barrier((copies_of(sketch, 16), sketch))
    blocks = swap(copies, ROW)
    band_block = from_first_column(sketch)
    received = swap(column_products(tiles, slots, place, band_block, False), ROW)
    row_part = row_products(tiles, slots, place, blocks, correction, sketch)
    band = to_first_column(over_cores(row_part))
    own = total(received) + jnp.where(first_col, band, 0.0)

    blocks = lax.all_gather(own, ROW, axis=0)
    gram = jnp.dot(own.T, own, precision=HIGHEST)
    both = jnp.concatenate([gram.reshape(16, 8, 128), own.reshape(16, 16, 128)], axis=1)
    both = swap(both, PLANE)
    lines = both[0, 8:]
    other = lax.ppermute(lines, "zh", [(0, 1)])
    lines = jnp.where(lax.axis_index("zh") == 0, lines, other)
    piece = total(swap(copies_of(total(both[:, :8]), 32), ACROSS))
    both = swap(copies_of(jnp.concatenate([piece, lines], axis=0), 16), PLANE)
    band_block, factor = normalise(both)

    placed = column_products(tiles, slots, place, band_block, True)
    received = total_of_four(swap(placed.reshape(4, 4, 256, 128), "x")).astype(jnp.bfloat16)
    received = swap(received, "zl")
    row_part = row_products(
        tiles, slots, place, blocks, correction, band_block, weight_of(factor)
    )
    col_sum = total_of_four(received)
    row_part = row_part + jnp.where(first_col, col_sum, 0.0)
    rest = jnp.where(first_col, 0.0, col_sum)
    band_rows = total(swap(row_part.reshape(32, 8, 128), COL))
    stacked = jnp.concatenate([rest, band_rows], axis=0)
    gram = jnp.dot(stacked.T, stacked, precision=HIGHEST)
    piece = total(swap(gram.reshape(16, 8, 128), PLANE))
    piece = total(swap(copies_of(piece, 32), ACROSS))
    other = lax.ppermute(band_rows, "zh", [(1, 0)])
    both = jnp.concatenate([piece, band_rows, other], axis=0)
    both = swap(copies_of(both, 16), PLANE)
    return normalise(both, col_id[None], rest)


def solution(mesh):
    fine = Mesh(mesh.devices.reshape(4, 4, 2, 8, 2), ROW + COL)
    in_specs = (
        P(None, ROW, COL, None, None),
        P(None, ROW, COL, None),
        P(COL + ROW, None),
    )
    return jax.shard_map(
        local, mesh=fine, in_specs=in_specs, out_specs=P(COL + ROW, None), check_vma=False
    )
```
